32 devices in a mesh: head: 4 (over y, core), ctx: 8 (over z, x).
Axes of the slice: x: 2, y: 2, z: 4, core: 2. Of those that a mesh axis runs over, the one named last changes fastest.
Arguments:
- main_queries: bfloat16 [256, 128, 192], P(None, 'head'), may hold values from -6 to 6
- main_keys: bfloat16 [8192, 128, 192], P('ctx', 'head'), may hold values from -7 to 7
- log_sums: float32 [256, 128], P(None, 'head'), may hold values from 10 to 13
- index_queries: bfloat16 [256, 64, 128], P('head'), may hold values from -2 to 2
- index_weights: bfloat16 [256, 64], P('head'), may hold values from -3 to 3
- index_keys: bfloat16 [8192, 128], P('ctx'), may hold values from -7 to 7
- loss_weights: float32 [256], P('head'), may hold values from 4 to 64
Outputs:
- query_grad: bfloat16 [256, 64, 128], P('head', 'ctx')
- weight_grad: float32 [256, 64], P('head', 'ctx')
- key_grad: bfloat16 [8192, 128], P('ctx', 'head')
The draws below stay inside these ranges and needn't reach their ends.
All inputs are finite; a program needn't handle non-finite values.
Results may differ from the reference program's by a relative error of at most 0.023.
Values may be sent and summed in bfloat16 or wider, within the bound.
A program may use at most 128 MiB of HBM per device.

```python
import math
import jax
import jax.numpy as jnp
from jax import lax

H = 128
DS = 192
IH = 64
ID = 128
QUERIES = 256
KEYS = 8192
N_HEAD = 4


def indexer_fields(key):
    base = jax.random.fold_in(key, 71)
    key_one, key_two, key_three = jax.random.split(base, 3)
    position = jnp.arange(KEYS, dtype=jnp.float32) / KEYS
    rising = 0.5 + 1.5 * position
    keys = jnp.clip(jax.random.normal(key_one, (KEYS, ID), jnp.float32), -3.5, 3.5) * rising[:, None]
    queries = jnp.clip(jax.random.normal(key_two, (QUERIES, IH, ID), jnp.float32), -4.0, 4.0) * ID ** (-0.5)
    weights = jnp.clip(jax.random.normal(key_three, (QUERIES, IH), jnp.float32), -4.0, 4.0) * 0.14
    return (queries, keys, weights)


def draw_index_queries(key, part):
    return indexer_fields(key)[0].astype(jnp.bfloat16)


def draw_index_keys(key, part):
    return indexer_fields(key)[1].astype(jnp.bfloat16)


def draw_index_weights(key, part):
    return indexer_fields(key)[2].astype(jnp.bfloat16)


def draw_main_queries(key, part):
    noise_key = jax.random.fold_in(key, 41)
    values = jnp.clip(jax.random.normal(noise_key, (QUERIES, H, DS), jnp.float32), -6.0, 6.0)
    return values.astype(jnp.bfloat16)


def draw_main_keys(key, part):
    key_one = jax.random.fold_in(jax.random.fold_in(key, 29), 0)
    rising = 0.6 + jnp.arange(KEYS, dtype=jnp.float32) / KEYS
    values = jnp.clip(jax.random.normal(key_one, (KEYS, H, DS), jnp.float32), -4.0, 4.0) * rising[:, None, None]
    return values.astype(jnp.bfloat16)


def levels(stream_key, dims, cuts, least, high):
    loudness, own = 1.0, jax.random.fold_in(stream_key, 6)
    for axis_at, blocks in cuts:
        draws = jnp.exp(jax.random.uniform(jax.random.fold_in(own, axis_at), (blocks,), jnp.float32, least / len(cuts), high / len(cuts)))
        loudness = loudness * jnp.repeat(draws, dims[axis_at] // blocks).reshape([-1 if axis == axis_at else 1 for axis in range(len(dims))])
    return loudness


def setup_inputs(seed: int = 0) -> dict:
    seeds = jax.random.split(jax.random.key(seed), 8)
    return {
        "main_queries": draw_main_queries(jax.random.fold_in(seeds[7], 71), 0),
        "main_keys": draw_main_keys(jax.random.fold_in(seeds[7], 71), 0),
        "log_sums": jnp.clip(10.0 + 3.0 * jax.random.uniform(seeds[2], (QUERIES, H), jnp.float32) ** levels(seeds[2], (QUERIES, H), ((1, 4),), -0.2, 0.2), 10.0, 13.0),
        "index_queries": draw_index_queries(jax.random.fold_in(seeds[7], 71), 0),
        "index_weights": draw_index_weights(jax.random.fold_in(seeds[7], 71), 0),
        "index_keys": draw_index_keys(jax.random.fold_in(seeds[7], 71), 0),
        "loss_weights": jnp.clip(jnp.exp(math.log(64.0) - 2.7725887 * jax.random.uniform(seeds[6], (QUERIES,), jnp.float32) ** levels(seeds[6], (QUERIES,), ((0, 4),), -0.2, 0.2)), 4.0, 64.0),
    }


def reference(main_queries, main_keys, log_sums, index_queries, index_weights, index_keys, loss_weights):
    score_scale = DS ** -0.5
    group_heads = H // N_HEAD
    block_rows = 8

    def head_prob(running, head_index):
        queries_one = lax.dynamic_index_in_dim(main_queries, head_index, 1, keepdims=False).astype(jnp.float32)
        keys_one = lax.dynamic_index_in_dim(main_keys, head_index, 1, keepdims=False).astype(jnp.float32)
        logs_one = lax.dynamic_index_in_dim(log_sums, head_index, 1, keepdims=False)
        scores = jnp.dot(queries_one, keys_one.T, preferred_element_type=jnp.float32) * score_scale
        return running + jnp.exp(scores - logs_one[:, None]), None

    def group_prob(running, group_index):
        head_list = group_index * group_heads + jnp.arange(group_heads, dtype=jnp.int32)
        partial_sum, ignored = lax.scan(head_prob, jnp.zeros((QUERIES, KEYS), jnp.float32), head_list)
        rounded = lax.optimization_barrier(partial_sum.astype(jnp.bfloat16))
        return running + rounded.astype(jnp.float32), None

    probs, ignored = lax.scan(group_prob, jnp.zeros((QUERIES, KEYS), jnp.float32), jnp.arange(N_HEAD, dtype=jnp.int32))
    keys_wide = index_keys.astype(jnp.float32)

    def query_block(key_total, block_index):
        first_row = (block_index * block_rows).astype(jnp.int32)
        queries_block = lax.dynamic_slice_in_dim(index_queries, first_row, block_rows, 0).astype(jnp.float32).reshape(block_rows * IH, ID)
        weights_block = lax.dynamic_slice_in_dim(index_weights, first_row, block_rows, 0).astype(jnp.float32)
        probs_block = lax.dynamic_slice_in_dim(probs, first_row, block_rows, 0)
        scale_block = lax.dynamic_slice_in_dim(loss_weights, first_row, block_rows, 0)
        raw_scores = jnp.dot(queries_block, keys_wide.T, preferred_element_type=jnp.float32).reshape(block_rows, IH, KEYS)
        positive = jnp.maximum(raw_scores, 0.0)
        logits = jnp.sum(weights_block[:, :, None] * positive, axis=1)
        row_top = jnp.max(logits, axis=1, keepdims=True)
        expo = jnp.exp(logits - row_top)
        soft_share = expo / jnp.sum(expo, axis=1, keepdims=True)
        target = probs_block / jnp.sum(probs_block, axis=1, keepdims=True)
        grad_rounded = lax.optimization_barrier((scale_block[:, None] * (soft_share - target)).astype(jnp.bfloat16))
        grad_logits = grad_rounded.astype(jnp.float32)
        weight_part = jnp.sum(grad_logits[:, None, :] * positive, axis=2)
        gated_rounded = lax.optimization_barrier(jnp.where(raw_scores > 0, grad_logits[:, None, :] * weights_block[:, :, None], 0.0).astype(jnp.bfloat16))
        gated_flat = gated_rounded.astype(jnp.float32).reshape(block_rows * IH, KEYS)
        query_part = jnp.dot(gated_flat, keys_wide, preferred_element_type=jnp.float32).reshape(block_rows, IH, ID)
        key_total = key_total + jnp.dot(gated_flat.T, queries_block, preferred_element_type=jnp.float32)
        return key_total, (query_part.astype(jnp.bfloat16), weight_part)

    key_total, (query_parts, weight_parts) = lax.scan(query_block, jnp.zeros((KEYS, ID), jnp.float32), jnp.arange(QUERIES // block_rows, dtype=jnp.int32))
    query_grad = query_parts.reshape(QUERIES, IH, ID)
    weight_grad = weight_parts.reshape(QUERIES, IH)
    return query_grad, weight_grad, key_total.astype(jnp.bfloat16)
```

```python
import functools
import math

import jax
import jax.numpy as jnp
from jax import lax
from jax.experimental import pallas as pl
from jax.experimental.pallas import tpu as pltpu
from jax.sharding import PartitionSpec as P

MESH = pl.DeviceIdType.MESH
F32 = jnp.float32
BF16 = jnp.bfloat16
KEY_CHUNK = 256
LANES = 128


def column(values, index):
    lane = lax.broadcasted_iota(jnp.int32, values.shape, 1)
    return jnp.sum(jnp.where(lane == index, values, 0.0), axis=1, keepdims=True)


def kernel(
    n_head, n_ctx,
    q_ref, k_ref, ls_ref, iq_ref, iw_ref, ik_ref, lw_ref,
    out_q, out_w, out_k,
    q_raw, q_rows, k_buf, acc, group_buf, group_in, raw_buf, logits, probs, grad,
    flip, stat_buf, stat_in, m_buf, m_in, key_acc, key_buf, key_in,
    q_sem, k_sem, group_send, group_recv, stat_send, stat_recv, m_send, m_recv, key_send, key_recv,
):
    me_h, me_c = lax.axis_index("head"), lax.axis_index("ctx")
    heads, width, all_queries = q_ref.shape
    keys = k_ref.shape[2]
    rows = lw_ref.shape[1]
    index_heads = iw_ref.shape[1]
    depth = k_buf.shape[1]
    own_heads = index_heads // n_ctx
    block = own_heads * rows
    features = out_k.shape[0]
    chunks = keys // KEY_CHUNK
    scale = width ** (-0.5)
    factor = scale * math.log2(math.e)

    q_copy = pltpu.make_async_copy(q_ref, q_raw, q_sem)
    q_copy.start()
    key_copies = []
    for c in range(chunks):
        part = pl.ds(c * KEY_CHUNK, KEY_CHUNK)
        copy = pltpu.make_async_copy(
            k_ref.at[:, :, part], k_buf.at[:, pl.ds(0, width), part], k_sem.at[c]
        )
        copy.start()
        key_copies.append(copy)

    barrier = pltpu.get_barrier_semaphore()
    for o in range(1, n_head):
        pl.semaphore_signal(
            barrier, inc=1, device_id={"head": lax.rem(me_h + o, n_head)}, device_id_type=MESH
        )
    for o in range(1, n_ctx):
        pl.semaphore_signal(
            barrier, inc=1, device_id={"ctx": lax.rem(me_c + o, n_ctx)}, device_id_type=MESH
        )

    k_buf[:, width:, :] = jnp.ones((heads, depth - width, keys), BF16)
    logits[...] = jnp.zeros_like(logits)
    key_acc[...] = jnp.zeros_like(key_acc)
    q_copy.wait()

    def turn(h, carry):
        saved = ls_ref[pl.ds(h, 1), :] * (-1.0 / scale)
        high = saved.astype(BF16).astype(F32)
        middle = (saved - high).astype(BF16).astype(F32)
        low = saved - high - middle
        place = lax.broadcasted_iota(jnp.int32, (depth - width, all_queries), 0)
        extra = jnp.where(
            place == 0, high, jnp.where(place == 1, middle, jnp.where(place == 2, low, 0.0))
        ).astype(BF16)
        q_rows[h] = jnp.concatenate([q_raw[h], extra], axis=0).T
        return carry

    lax.fori_loop(0, heads, turn, 0)
    pl.semaphore_wait(barrier, n_head + n_ctx - 2)

    def group_copy(c, o):
        dest = lax.rem(me_h + o, n_head)
        return pltpu.make_async_remote_copy(
            src_ref=group_buf.at[c, pl.ds(pl.multiple_of(dest * rows, rows), rows), :],
            dst_ref=group_in.at[c, o - 1],
            send_sem=group_send.at[c, o - 1],
            recv_sem=group_recv.at[c, o - 1],
            device_id={"head": dest},
            device_id_type=MESH,
        )

    step_heads = 4 if heads % 4 == 0 else 1
    for c in range(chunks):
        key_copies[c].wait()
        acc[...] = jnp.zeros_like(acc)

        def some_heads(i, carry, c=c):
            total = None
            for u in range(step_heads):
                h = i * step_heads + u
                scores = jnp.dot(
                    q_rows[h],
                    k_buf[h, :, c * KEY_CHUNK : (c + 1) * KEY_CHUNK],
                    preferred_element_type=F32,
                )
                part = jnp.exp2(scores * factor)
                total = part if total is None else total + part
            acc[...] += total
            return carry

        lax.fori_loop(0, heads // step_heads, some_heads, 0)
        group_buf[c] = acc[...].astype(BF16)
        for o in range(1, n_head):
            group_copy(c, o).start()

    weights = iw_ref[...].astype(F32)
    tile = min(256, block)
    tile_heads = tile // rows

    def logit_step(i, carry):
        part = pl.ds(pl.multiple_of(i * tile, tile), tile)
        queries = iq_ref[part, :]
        cols = [column(weights, i * tile_heads + u) for u in range(tile_heads)]
        for c in range(chunks):
            span = slice(c * KEY_CHUNK, (c + 1) * KEY_CHUNK)
            raw = lax.dot_general(
                queries, ik_ref[span, :], (((1,), (1,)), ((), ())), preferred_element_type=F32
            )
            raw_buf[part, span] = raw.astype(BF16)
            total = logits[:, span]
            for u in range(tile_heads):
                total += cols[u] * jnp.maximum(raw[u * rows : (u + 1) * rows], 0.0)
            logits[:, span] = total
        return carry

    lax.fori_loop(0, index_heads // tile_heads, logit_step, 0)
    values = logits[...]
    top = jnp.max(values, axis=1, keepdims=True)
    total = jnp.sum(jnp.exp(values - top), axis=1, keepdims=True)

    mine = pl.ds(pl.multiple_of(me_h * rows, rows), rows)
    mass = jnp.zeros((rows, 1), F32)
    for c in range(chunks):
        summed = group_buf[c, mine, :].astype(F32)
        for o in range(1, n_head):
            group_copy(c, o).wait_recv()
            summed += group_in[c, o - 1].astype(F32)
        probs[:, c * KEY_CHUNK : (c + 1) * KEY_CHUNK] = summed
        mass += jnp.sum(summed, axis=1, keepdims=True)

    flip[...] = jnp.zeros_like(flip)
    lane = lax.broadcasted_iota(jnp.int32, (rows, LANES), 1)
    flip[0:rows, :] = jnp.where(
        lane == 0, top, jnp.where(lane == 1, total, jnp.where(lane == 2, mass, 0.0))
    )
    stat_buf[...] = flip[...].T[0:8, :]

    def stat_copy(o):
        return pltpu.make_async_remote_copy(
            src_ref=stat_buf,
            dst_ref=stat_in.at[o - 1],
            send_sem=stat_send.at[o - 1],
            recv_sem=stat_recv.at[o - 1],
            device_id={"ctx": lax.rem(me_c + o, n_ctx)},
            device_id_type=MESH,
        )

    for o in range(1, n_ctx):
        stat_copy(o).start()
    own = stat_buf[...]
    stats = [own]
    for o in range(1, n_ctx):
        stat_copy(o).wait_recv()
        stats.append(stat_in[o - 1])
    all_top = functools.reduce(jnp.maximum, [s[0:1] for s in stats])
    all_total = sum(s[1:2] * jnp.exp(s[0:1] - all_top) for s in stats)
    all_mass = sum(s[2:3] for s in stats)
    flip[0:1, :] = all_top
    flip[1:2, :] = 1.0 / all_total
    flip[2:3, :] = 1.0 / all_mass
    flip[3:4, 0:rows] = lw_ref[...]
    back = flip[...].T[0:rows, :]
    top, per_total, per_mass, loss = (back[:, i : i + 1] for i in range(4))
    soft = jnp.exp(logits[...] - top) * per_total
    grad[...] = (loss * (soft - probs[...] * per_mass)).astype(BF16)

    def m_copy(o):
        dest = lax.rem(me_c + o + 1, n_ctx)
        return pltpu.make_async_remote_copy(
            src_ref=m_buf.at[pl.ds(pl.multiple_of(dest * block, block), block), :],
            dst_ref=m_in.at[o],
            send_sem=m_send.at[o],
            recv_sem=m_recv.at[o],
            device_id={"ctx": dest},
            device_id_type=MESH,
        )

    def grad_step(o, carry):
        dest = lax.rem(me_c + o + 1, n_ctx)
        for v in range(block // tile):
            start = pl.multiple_of(dest * block + v * tile, tile)
            part = pl.ds(start, tile)
            queries = iq_ref[part, :].astype(F32)
            first = dest * own_heads + v * tile_heads
            scaled = jnp.concatenate(
                [
                    queries[u * rows : (u + 1) * rows] * column(weights, first + u)
                    for u in range(tile_heads)
                ],
                axis=0,
            )
            gated = jnp.concatenate(
                [
                    jnp.where(
                        raw_buf[pl.ds(start + u * rows, rows), :] > 0, grad[...], jnp.zeros((), BF16)
                    )
                    for u in range(tile_heads)
                ],
                axis=0,
            )
            m_buf[part, :] = jnp.dot(gated, ik_ref[...], preferred_element_type=F32).astype(BF16)
            key_acc[...] += jnp.dot(scaled.T.astype(BF16), gated, preferred_element_type=F32)

        @pl.when(o < n_ctx - 1)
        def _():
            m_copy(o).start()

        return carry

    lax.fori_loop(0, n_ctx, grad_step, 0)

    key_buf[...] = key_acc[...].astype(BF16)

    def key_copy(o):
        dest = lax.rem(me_h + o, n_head)
        return pltpu.make_async_remote_copy(
            src_ref=key_buf.at[pl.ds(pl.multiple_of(dest * features, features), features), :],
            dst_ref=key_in.at[o - 1],
            send_sem=key_send.at[o - 1],
            recv_sem=key_recv.at[o - 1],
            device_id={"head": dest},
            device_id_type=MESH,
        )

    for o in range(1, n_head):
        key_copy(o).start()
    key_total = key_buf[pl.ds(pl.multiple_of(me_h * features, features), features), :].astype(F32)
    for o in range(1, n_head):
        key_copy(o).wait_recv()
        key_total += key_in[o - 1].astype(F32)
    out_k[...] = key_total.astype(BF16)

    own_rows = pl.ds(pl.multiple_of(me_c * block, block), block)
    m_total = m_buf[own_rows, :].astype(F32)
    for o in range(n_ctx - 1):
        m_copy(o).wait_recv()
        m_total += m_in[o].astype(F32)
    dots = iq_ref[own_rows, :].astype(F32) * m_total
    place = lax.broadcasted_iota(jnp.int32, (rows, own_heads), 1)
    weight_total = jnp.zeros((rows, own_heads), F32)
    for u in range(own_heads):
        span = slice(u * rows, (u + 1) * rows)
        col = column(weights, me_c * own_heads + u)
        out_q[u] = (m_total[span] * col).astype(BF16)
        weight_total = jnp.where(
            place == u, jnp.sum(dots[span], axis=1, keepdims=True), weight_total
        )
    out_w[...] = weight_total

    for c in range(chunks):
        for o in range(1, n_head):
            group_copy(c, o).wait_send()
    for o in range(1, n_ctx):
        stat_copy(o).wait_send()
    for o in range(n_ctx - 1):
        m_copy(o).wait_send()
    for o in range(1, n_head):
        key_copy(o).wait_send()


def per_device(
    n_head, n_ctx,
    main_queries, main_keys, log_sums, index_queries, index_weights, index_keys, loss_weights,
):
    all_queries, heads, width = main_queries.shape
    keys = main_keys.shape[0]
    rows, index_heads, size = index_queries.shape
    own_heads = index_heads // n_ctx
    features = size // n_head
    depth = (width + 16 + LANES - 1) // LANES * LANES
    chunks = keys // KEY_CHUNK
    flat = rows * index_heads
    queries = index_queries.transpose(1, 0, 2).reshape(flat, size)
    vmem = pl.BlockSpec(memory_space=pltpu.VMEM)
    hbm = pl.BlockSpec(memory_space=pl.ANY)
    dma = pltpu.SemaphoreType.DMA
    query_grad, weight_grad, key_grad = pl.pallas_call(
        functools.partial(kernel, n_head, n_ctx),
        out_shape=(
            jax.ShapeDtypeStruct((own_heads, rows, size), BF16),
            jax.ShapeDtypeStruct((rows, own_heads), F32),
            jax.ShapeDtypeStruct((features, keys), BF16),
        ),
        in_specs=[hbm, hbm, vmem, vmem, vmem, vmem, vmem],
        out_specs=(vmem, vmem, vmem),
        scratch_shapes=[
            pltpu.VMEM((heads, width, all_queries), BF16),
            pltpu.VMEM((heads, all_queries, depth), BF16),
            pltpu.VMEM((heads, depth, keys), BF16),
            pltpu.VMEM((all_queries, KEY_CHUNK), F32),
            pltpu.VMEM((chunks, all_queries, KEY_CHUNK), BF16),
            pltpu.VMEM((chunks, n_head - 1, rows, KEY_CHUNK), BF16),
            pltpu.VMEM((flat, keys), BF16),
            pltpu.VMEM((rows, keys), F32),
            pltpu.VMEM((rows, keys), F32),
            pltpu.VMEM((rows, keys), BF16),
            pltpu.VMEM((LANES, LANES), F32),
            pltpu.VMEM((8, LANES), F32),
            pltpu.VMEM((n_ctx - 1, 8, LANES), F32),
            pltpu.VMEM((flat, size), BF16),
            pltpu.VMEM((n_ctx - 1, own_heads * rows, size), BF16),
            pltpu.VMEM((size, keys), F32),
            pltpu.VMEM((size, keys), BF16),
            pltpu.VMEM((n_head - 1, features, keys), BF16),
            dma, dma((chunks,)),
            dma((chunks, n_head - 1)), dma((chunks, n_head - 1)),
            dma((n_ctx - 1,)), dma((n_ctx - 1,)),
            dma((n_ctx - 1,)), dma((n_ctx - 1,)),
            dma((n_head - 1,)), dma((n_head - 1,)),
        ],
        compiler_params=pltpu.CompilerParams(
            collective_id=0, has_side_effects=True, vmem_limit_bytes=56 * 1024 * 1024
        ),
        name="indexer_backward",
    )(
        main_queries.transpose(1, 2, 0),
        main_keys.transpose(1, 2, 0),
        log_sums.T,
        queries,
        index_weights,
        index_keys,
        loss_weights.reshape(1, rows),
    )
    return query_grad.transpose(1, 0, 2), weight_grad, key_grad.T


def solution(mesh):
    return jax.shard_map(
        functools.partial(per_device, mesh.shape["head"], mesh.shape["ctx"]),
        mesh=mesh,
        in_specs=(
            P(None, "head", None),
            P("ctx", "head", None),
            P(None, "head"),
            P("head", None, None),
            P("head", None),
            P("ctx", None),
            P("head"),
        ),
        out_specs=(P("head", "ctx", None), P("head", "ctx"), P("ctx", "head")),
        check_vma=False,
    )
```

```python
import functools
import math

import jax
import jax.numpy as jnp
from jax import lax
from jax.experimental import pallas as pl
from jax.experimental.pallas import tpu as pltpu
from jax.sharding import PartitionSpec as P

MESH = pl.DeviceIdType.MESH
F32 = jnp.float32
BF16 = jnp.bfloat16
KEY_CHUNK = 256
LANES = 128


def column(values, index):
    lane = lax.broadcasted_iota(jnp.int32, values.shape, 1)
    return jnp.sum(jnp.where(lane == index, values, 0.0), axis=1, keepdims=True)


def kernel(
    n_head, n_ctx,
    q_ref, k_ref, ls_ref, iq_in, iw_ref, ik_ref, lw_ref,
    out_q, out_w, out_k,
    q_raw, q_rows, k_buf, acc, group_buf, group_in, raw_buf, logits, probs, grad,
    flip, stat_buf, stat_in, iq_ref, m_buf, p_in, m_in, key_acc, key_buf, key_in,
    q_sem, k_sem, group_send, group_recv, stat_send, stat_recv, p_send, p_recv, m_send, m_recv, key_send, key_recv,
):
    me_h, me_c = lax.axis_index("head"), lax.axis_index("ctx")
    heads, width, all_queries = q_ref.shape
    keys = k_ref.shape[2]
    rows = lw_ref.shape[1]
    index_heads = iw_ref.shape[1]
    depth = k_buf.shape[1]
    own_heads = index_heads // n_ctx
    block = own_heads * rows
    features = out_k.shape[0]
    size = ik_ref.shape[1]
    chunks = keys // KEY_CHUNK
    scale = width ** (-0.5)
    factor = scale * math.log2(math.e)

    q_copy = pltpu.make_async_copy(q_ref, q_raw, q_sem)
    q_copy.start()
    key_copies = []
    for c in range(chunks):
        part = pl.ds(c * KEY_CHUNK, KEY_CHUNK)
        copy = pltpu.make_async_copy(
            k_ref.at[:, :, part], k_buf.at[:, pl.ds(0, width), part], k_sem.at[c]
        )
        copy.start()
        key_copies.append(copy)

    barrier = pltpu.get_barrier_semaphore()
    for o in range(1, n_head):
        pl.semaphore_signal(
            barrier, inc=1, device_id={"head": lax.rem(me_h + o, n_head)}, device_id_type=MESH
        )
    for o in range(1, n_ctx):
        pl.semaphore_signal(
            barrier, inc=1, device_id={"ctx": lax.rem(me_c + o, n_ctx)}, device_id_type=MESH
        )

    k_buf[:, width:, :] = jnp.ones((heads, depth - width, keys), BF16)
    logits[...] = jnp.zeros_like(logits)
    key_acc[...] = jnp.zeros_like(key_acc)
    iq_ref[...] = (
        jnp.swapaxes(iq_in[...].astype(F32), 0, 1).reshape(iq_ref.shape).astype(BF16)
    )
    q_copy.wait()

    def turn(h, carry):
        saved = ls_ref[pl.ds(h, 1), :] * (-1.0 / scale)
        high = saved.astype(BF16).astype(F32)
        middle = (saved - high).astype(BF16).astype(F32)
        low = saved - high - middle
        place = lax.broadcasted_iota(jnp.int32, (depth - width, all_queries), 0)
        extra = jnp.where(
            place == 0, high, jnp.where(place == 1, middle, jnp.where(place == 2, low, 0.0))
        ).astype(BF16)
        q_rows[h] = jnp.concatenate([q_raw[h], extra], axis=0).T
        return carry

    lax.fori_loop(0, heads, turn, 0)
    pl.semaphore_wait(barrier, n_head + n_ctx - 2)

    def group_copy(c, o):
        dest = lax.rem(me_h + o, n_head)
        return pltpu.make_async_remote_copy(
            src_ref=group_buf.at[c, pl.ds(pl.multiple_of(dest * rows, rows), rows), :],
            dst_ref=group_in.at[c, o - 1],
            send_sem=group_send.at[c, o - 1],
            recv_sem=group_recv.at[c, o - 1],
            device_id={"head": dest},
            device_id_type=MESH,
        )

    weights = iw_ref[...].astype(F32)
    tile = min(256, block)
    tile_heads = tile // rows

    def logit_step(i, carry):
        part = pl.ds(pl.multiple_of(i * tile, tile), tile)
        queries = iq_ref[part, :]
        cols = [column(weights, i * tile_heads + u) for u in range(tile_heads)]
        for c in range(chunks):
            span = slice(c * KEY_CHUNK, (c + 1) * KEY_CHUNK)
            raw = lax.dot_general(
                queries, ik_ref[span, :], (((1,), (1,)), ((), ())), preferred_element_type=F32
            )
            raw_buf[part, span] = raw.astype(BF16)
            total = logits[:, span]
            for u in range(tile_heads):
                total += cols[u] * jnp.maximum(raw[u * rows : (u + 1) * rows], 0.0)
            logits[:, span] = total
        return carry

    logit_steps = index_heads // tile_heads
    lax.fori_loop(0, logit_steps // 2, logit_step, 0)

    step_heads = 4 if heads % 4 == 0 else 1
    for c in range(chunks):
        key_copies[c].wait()
        acc[...] = jnp.zeros_like(acc)

        def some_heads(i, carry, c=c):
            total = None
            for u in range(step_heads):
                h = i * step_heads + u
                scores = jnp.dot(
                    q_rows[h],
                    k_buf[h, :, c * KEY_CHUNK : (c + 1) * KEY_CHUNK],
                    preferred_element_type=F32,
                )
                part = jnp.exp2(scores * factor)
                total = part if total is None else total + part
            acc[...] += total
            return carry

        lax.fori_loop(0, heads // step_heads, some_heads, 0)
        group_buf[c] = acc[...].astype(BF16)
        for o in range(1, n_head):
            group_copy(c, o).start()

    lax.fori_loop(logit_steps // 2, logit_steps, logit_step, 0)
    values = logits[...]
    top = jnp.max(values, axis=1, keepdims=True)
    total = jnp.sum(jnp.exp(values - top), axis=1, keepdims=True)

    mine = pl.ds(pl.multiple_of(me_h * rows, rows), rows)
    mass = jnp.zeros((rows, 1), F32)
    for c in range(chunks):
        summed = group_buf[c, mine, :].astype(F32)
        for o in range(1, n_head):
            group_copy(c, o).wait_recv()
            summed += group_in[c, o - 1].astype(F32)
        probs[:, c * KEY_CHUNK : (c + 1) * KEY_CHUNK] = summed
        mass += jnp.sum(summed, axis=1, keepdims=True)

    flip[...] = jnp.zeros_like(flip)
    lane = lax.broadcasted_iota(jnp.int32, (rows, LANES), 1)
    flip[0:rows, :] = jnp.where(
        lane == 0, top, jnp.where(lane == 1, total, jnp.where(lane == 2, mass, 0.0))
    )
    stat_buf[...] = flip[...].T[0:8, :]

    def stat_copy(o):
        return pltpu.make_async_remote_copy(
            src_ref=stat_buf,
            dst_ref=stat_in.at[o - 1],
            send_sem=stat_send.at[o - 1],
            recv_sem=stat_recv.at[o - 1],
            device_id={"ctx": lax.rem(me_c + o, n_ctx)},
            device_id_type=MESH,
        )

    for o in range(1, n_ctx):
        stat_copy(o).start()
    own = stat_buf[...]
    stats = [own]
    for o in range(1, n_ctx):
        stat_copy(o).wait_recv()
        stats.append(stat_in[o - 1])
    all_top = functools.reduce(jnp.maximum, [s[0:1] for s in stats])
    all_total = sum(s[1:2] * jnp.exp(s[0:1] - all_top) for s in stats)
    all_mass = sum(s[2:3] for s in stats)
    flip[0:1, :] = all_top
    flip[1:2, :] = 1.0 / all_total
    flip[2:3, :] = 1.0 / all_mass
    flip[3:4, 0:rows] = lw_ref[...]
    back = flip[...].T[0:rows, :]
    top, per_total, per_mass, loss = (back[:, i : i + 1] for i in range(4))
    soft = jnp.exp(logits[...] - top) * per_total
    grad[...] = (loss * (soft - probs[...] * per_mass)).astype(BF16)

    pairs = n_ctx // 2
    side = lax.rem(me_c, 2)
    pair = me_c // 2

    def rows_of(i, other):
        dest = lax.rem(pair + i + 1, pairs) * 2 + (1 - side if other else side)
        return dest, pl.ds(pl.multiple_of(dest * block, block), block)

    def p_copy(i):
        return pltpu.make_async_remote_copy(
            src_ref=m_buf.at[rows_of(i, True)[1], :],
            dst_ref=p_in.at[i],
            send_sem=p_send.at[i],
            recv_sem=p_recv.at[i],
            device_id={"ctx": pair * 2 + 1 - side},
            device_id_type=MESH,
        )

    def m_copy(i):
        dest, part = rows_of(i, False)
        return pltpu.make_async_remote_copy(
            src_ref=m_buf.at[part, :],
            dst_ref=m_in.at[i],
            send_sem=m_send.at[i],
            recv_sem=m_recv.at[i],
            device_id={"ctx": dest},
            device_id_type=MESH,
        )

    def join(i):
        part = rows_of(i, False)[1]
        p_copy(i).wait_recv()
        m_buf[part, :] = (m_buf[part, :].astype(F32) + p_in[i].astype(F32)).astype(BF16)

    def grad_block(dest):
        for v in range(block // tile):
            start = pl.multiple_of(dest * block + v * tile, tile)
            part = pl.ds(start, tile)
            queries = iq_ref[part, :].astype(F32)
            first = dest * own_heads + v * tile_heads
            scaled = jnp.concatenate(
                [
                    queries[u * rows : (u + 1) * rows] * column(weights, first + u)
                    for u in range(tile_heads)
                ],
                axis=0,
            )
            gated = jnp.concatenate(
                [
                    jnp.where(
                        raw_buf[pl.ds(start + u * rows, rows), :] > 0, grad[...], jnp.zeros((), BF16)
                    )
                    for u in range(tile_heads)
                ],
                axis=0,
            )
            m_buf[part, :] = jnp.dot(gated, ik_ref[...], preferred_element_type=F32).astype(BF16)
            key_acc[...] += jnp.dot(scaled.T.astype(BF16), gated, preferred_element_type=F32)

    def other_side(i, carry):
        grad_block(rows_of(i, True)[0])
        p_copy(i).start()
        return carry

    def own_side(i, carry):
        grad_block(rows_of(i, False)[0])

        @pl.when(jnp.logical_and(i == 0, pairs > 1))
        def _():
            join(i)
            m_copy(i).start()

        return carry

    lax.fori_loop(0, pairs, other_side, 0)
    lax.fori_loop(0, pairs, own_side, 0)

    key_buf[...] = key_acc[...].astype(BF16)

    def key_copy(o):
        dest = lax.rem(me_h + o, n_head)
        return pltpu.make_async_remote_copy(
            src_ref=key_buf.at[pl.ds(pl.multiple_of(dest * features, features), features), :],
            dst_ref=key_in.at[o - 1],
            send_sem=key_send.at[o - 1],
            recv_sem=key_recv.at[o - 1],
            device_id={"head": dest},
            device_id_type=MESH,
        )

    for o in range(1, n_head):
        key_copy(o).start()
    for i in range(1, pairs):
        join(i)
        if i < pairs - 1:
            m_copy(i).start()
    key_total = key_buf[pl.ds(pl.multiple_of(me_h * features, features), features), :].astype(F32)
    for o in range(1, n_head):
        key_copy(o).wait_recv()
        key_total += key_in[o - 1].astype(F32)
    out_k[...] = key_total.astype(BF16)

    own_rows = pl.ds(pl.multiple_of(me_c * block, block), block)
    m_total = m_buf[own_rows, :].astype(F32)
    for i in range(pairs - 1):
        m_copy(i).wait_recv()
        m_total += m_in[i].astype(F32)
    dots = iq_ref[own_rows, :].astype(F32) * m_total
    flip[...] = jnp.zeros_like(flip)
    weight_total = flip[0:rows, :]
    grads = []
    for u in range(own_heads):
        span = slice(u * rows, (u + 1) * rows)
        grads.append(m_total[span] * column(weights, me_c * own_heads + u))
        weight_total = jnp.where(
            lane == u, jnp.sum(dots[span], axis=1, keepdims=True), weight_total
        )
    out_q[...] = jnp.swapaxes(
        jnp.concatenate(grads, axis=0).reshape(own_heads, rows, size), 0, 1
    ).astype(BF16)
    flip[0:rows, :] = weight_total
    out_w[...] = flip[...].T[0:own_heads, 0:rows]

    for c in range(chunks):
        for o in range(1, n_head):
            group_copy(c, o).wait_send()
    for o in range(1, n_ctx):
        stat_copy(o).wait_send()
    for i in range(pairs):
        p_copy(i).wait_send()
    for i in range(pairs - 1):
        m_copy(i).wait_send()
    for o in range(1, n_head):
        key_copy(o).wait_send()


def hand_out(q_in, w_in, k_in, q_out, w_out, k_out):
    q_out[...] = q_in[...]
    w_out[...] = w_in[...]
    k_out[...] = k_in[...]


def per_device(
    n_head, n_ctx,
    main_queries, main_keys, log_sums, index_queries, index_weights, index_keys, loss_weights,
):
    all_queries, heads, width = main_queries.shape
    keys = main_keys.shape[0]
    rows, index_heads, size = index_queries.shape
    own_heads = index_heads // n_ctx
    features = size // n_head
    depth = (width + 16 + LANES - 1) // LANES * LANES
    chunks = keys // KEY_CHUNK
    flat = rows * index_heads
    pairs = n_ctx // 2
    vmem = pl.BlockSpec(memory_space=pltpu.VMEM)
    hbm = pl.BlockSpec(memory_space=pl.ANY)
    dma = pltpu.SemaphoreType.DMA
    query_grad, weight_grad, key_grad = pl.pallas_call(
        functools.partial(kernel, n_head, n_ctx),
        out_shape=(
            jax.ShapeDtypeStruct((rows, own_heads, size), BF16),
            jax.ShapeDtypeStruct((own_heads, rows), F32),
            jax.ShapeDtypeStruct((features, keys), BF16),
        ),
        in_specs=[hbm, hbm, vmem, vmem, vmem, vmem, vmem],
        out_specs=(vmem, vmem, vmem),
        scratch_shapes=[
            pltpu.VMEM((heads, width, all_queries), BF16),
            pltpu.VMEM((heads, all_queries, depth), BF16),
            pltpu.VMEM((heads, depth, keys), BF16),
            pltpu.VMEM((all_queries, KEY_CHUNK), F32),
            pltpu.VMEM((chunks, all_queries, KEY_CHUNK), BF16),
            pltpu.VMEM((chunks, n_head - 1, rows, KEY_CHUNK), BF16),
            pltpu.VMEM((flat, keys), BF16),
            pltpu.VMEM((rows, keys), F32),
            pltpu.VMEM((rows, keys), F32),
            pltpu.VMEM((rows, keys), BF16),
            pltpu.VMEM((LANES, LANES), F32),
            pltpu.VMEM((8, LANES), F32),
            pltpu.VMEM((n_ctx - 1, 8, LANES), F32),
            pltpu.VMEM((flat, size), BF16),
            pltpu.VMEM((flat, size), BF16),
            pltpu.VMEM((pairs, own_heads * rows, size), BF16),
            pltpu.VMEM((pairs - 1, own_heads * rows, size), BF16),
            pltpu.VMEM((size, keys), F32),
            pltpu.VMEM((size, keys), BF16),
            pltpu.VMEM((n_head - 1, features, keys), BF16),
            dma, dma((chunks,)),
            dma((chunks, n_head - 1)), dma((chunks, n_head - 1)),
            dma((n_ctx - 1,)), dma((n_ctx - 1,)),
            dma((pairs,)), dma((pairs,)),
            dma((pairs - 1,)), dma((pairs - 1,)),
            dma((n_head - 1,)), dma((n_head - 1,)),
        ],
        compiler_params=pltpu.CompilerParams(
            collective_id=0, has_side_effects=True, vmem_limit_bytes=56 * 1024 * 1024
        ),
        name="indexer_backward",
    )(
        main_queries.transpose(1, 2, 0),
        main_keys.transpose(1, 2, 0),
        log_sums.T,
        index_queries,
        index_weights,
        index_keys,
        loss_weights.reshape(1, rows),
    )
    results = (query_grad, weight_grad, key_grad)
    query_grad, weight_grad, key_grad = pl.pallas_call(
        hand_out,
        out_shape=tuple(jax.ShapeDtypeStruct(x.shape, x.dtype) for x in results),
        in_specs=[vmem] * 3,
        out_specs=(vmem,) * 3,
        name="hand_out",
    )(*results)
    return query_grad, weight_grad.T, key_grad.T


def solution(mesh):
    return jax.shard_map(
        functools.partial(per_device, mesh.shape["head"], mesh.shape["ctx"]),
        mesh=mesh,
        in_specs=(
            P(None, "head", None),
            P("ctx", "head", None),
            P(None, "head"),
            P("head", None, None),
            P("head", None),
            P("ctx", None),
            P("head"),
        ),
        out_specs=(P("head", "ctx", None), P("head", "ctx"), P("ctx", "head")),
        check_vma=False,
    )
```
